512 devices in a mesh: tenant: 16 (over y_hi, z), feat: 32 (over y_lo, x, core).
Axes of the slice: x: 4, y: 8 (y_hi: 2, y_lo: 4; y = y_hi * 4 + y_lo), z: 8, core: 2. Of those that a mesh axis runs over, the one named last changes fastest.
Arguments:
- adapter_input_weight: float32 [512, 16, 8192], P('tenant', None, 'feat'), may hold values from -3 to 3
- adapter_output_weight: float32 [512, 16, 8192], P('tenant', None, 'feat'), may hold values from -3 to 3
- initial_output_basis: float32 [8192, 256], P('feat'), may hold values from -6 to 6
- initial_input_basis: float32 [8192, 256], P('feat'), may hold values from -6 to 6
Outputs:
- cores: float32 [512, 256, 256], P('tenant', 'feat')
- output_basis: float32 [8192, 256], P('feat')
- input_basis: float32 [8192, 256], P('feat')
The draws below stay inside these ranges and needn't reach their ends.
All inputs are finite; a program needn't handle non-finite values.
Results may differ from the reference program's by a relative error of at most 0.0003.
Values sent between devices are 32-bit elements; how exact they have to be, the bound alone decides.
No kernel may reach another device: no remote copies, remote signals or barrier semaphores. Data moves between devices by JAX's collectives and lax.ppermute only.
A program may use at most 64 MiB of HBM per device.

```python
import math
import jax
import jax.numpy as jnp
from jax import lax

PROJ_WIDTH = 8192
ADAPTER_RANK = 16
R = 256
ITERS = 2
TENANT_COUNT = 512


def level_of(rng, shape, shards, smallest, largest):
    factor_of = 1.0
    for axis_at, shards_of in shards:
        draws = jax.random.uniform(jax.random.fold_in(jax.random.fold_in(rng, 6), axis_at), (shards_of,), jnp.float32, smallest / len(shards), largest / len(shards))
        factor_of = factor_of * jnp.repeat(jnp.exp(draws), shape[axis_at] // shards_of).reshape((-1,) + (1,) * (len(shape) - 1 - axis_at))
    return factor_of


def scatter_about(own_key, shape, spread, limit, shards=(), dtype=jnp.bfloat16):
    drawn = jax.random.normal(own_key, shape, jnp.float32) * spread
    if len(shards) > 0:
        drawn = level_of(own_key, shape, shards, -0.22, 0.18) * drawn
    return jnp.clip(drawn, min=-limit, max=limit).astype(dtype)


def setup_inputs(seed: int = 0) -> dict:
    key_of = jax.random.split(jax.random.key(seed), 5)
    return {
        "adapter_input_weight": scatter_about(key_of[0], (TENANT_COUNT, ADAPTER_RANK, PROJ_WIDTH), 0.5, 3.0, ((0, 16), (2, 32)), jnp.float32),
        "adapter_output_weight": scatter_about(key_of[1], (TENANT_COUNT, ADAPTER_RANK, PROJ_WIDTH), 0.5, 3.0, ((0, 16), (2, 32)), jnp.float32),
        "initial_output_basis": scatter_about(key_of[2], (PROJ_WIDTH, R), 1.0, 6.0, ((0, 32),), jnp.float32),
        "initial_input_basis": scatter_about(key_of[3], (PROJ_WIDTH, R), 1.0, 6.0, ((0, 32),), jnp.float32),
    }


HIGH_PRECISION = lax.Precision.HIGHEST

def orthonormal(raw_basis):
    gram_matrix = jnp.dot(raw_basis.T, raw_basis, precision=HIGH_PRECISION) / PROJ_WIDTH
    lower_factor = jnp.linalg.cholesky(gram_matrix)
    return jax.scipy.linalg.solve_triangular(lower_factor, raw_basis.T, lower=True).T

def project_onto_basis(shared_basis, adapter_weights):
    return jnp.einsum('pyw,wj->pyj', adapter_weights, shared_basis, precision=HIGH_PRECISION) / math.sqrt(PROJ_WIDTH)

def reference(adapter_input_weight, adapter_output_weight, initial_output_basis, initial_input_basis):
    output_basis, input_basis = (initial_output_basis, initial_input_basis)
    for step in range(ITERS):
        projected_output = project_onto_basis(output_basis, adapter_output_weight)
        projected_input = project_onto_basis(input_basis, adapter_input_weight)
        gram_q = jnp.einsum('trk,tsk->trs', projected_input, projected_input, precision=HIGH_PRECISION)
        gram_p = jnp.einsum('trk,tsk->trs', projected_output, projected_output, precision=HIGH_PRECISION)
        output_factor = jnp.einsum('trs,tsk->trk', gram_q, projected_output, precision=HIGH_PRECISION)
        input_factor = jnp.einsum('trs,tsk->trk', gram_p, projected_input, precision=HIGH_PRECISION)
        updated_output_basis = jnp.einsum('hos,hol->sl', adapter_output_weight, output_factor, precision=HIGH_PRECISION)
        updated_input_basis = jnp.einsum('hos,hol->sl', adapter_input_weight, input_factor, precision=HIGH_PRECISION)
        output_basis = orthonormal(updated_output_basis)
        input_basis = orthonormal(updated_input_basis)
    projected_output = project_onto_basis(output_basis, adapter_output_weight)
    projected_input = project_onto_basis(input_basis, adapter_input_weight)
    cores = jnp.einsum('trk,trl->tkl', projected_output, projected_input, precision=HIGH_PRECISION)
    return (cores, output_basis, input_basis)
```

```python
import math

import jax
import jax.numpy as jnp
from jax import lax
from jax.sharding import PartitionSpec as P

PROJ_WIDTH = 8192
ITERS = 2
HIGH_PRECISION = lax.Precision.HIGHEST


def mm(a, b, ca, cb):
    return lax.dot_general(
        a, b, (((ca,), (cb,)), ((), ())), precision=HIGH_PRECISION,
        preferred_element_type=jnp.float32,
    )


def bmm(a, b, ca, cb):
    return lax.dot_general(
        a, b, (((ca,), (cb,)), ((0,), (0,))), precision=HIGH_PRECISION,
        preferred_element_type=jnp.float32,
    )


def scatter_sum(chunks, axis):
    return jnp.sum(lax.all_to_all(chunks, axis, 0, 0, tiled=True), axis=0)


def gather(own, axis):
    n = lax.axis_size(axis)
    return lax.all_to_all(
        jnp.broadcast_to(own[None], (n,) + own.shape), axis, 0, 0, tiled=True
    )


def inverse_factor(gram_matrix):
    lower_factor = jnp.linalg.cholesky(gram_matrix / PROJ_WIDTH)
    return jax.scipy.linalg.solve_triangular(
        lower_factor, jnp.eye(gram_matrix.shape[0], dtype=jnp.float32), lower=True
    )


def update(w_out, w_in, factor_out, factor_in):
    parts = jnp.stack([mm(w_out, factor_out, 0, 0), mm(w_in, factor_in, 0, 0)])
    n = lax.axis_size("tenant")
    two, feats, r = parts.shape
    chunks = parts.reshape(2, n, feats // n, r).transpose(1, 0, 2, 3)
    whole = gather(scatter_sum(chunks, "tenant"), "tenant")
    whole = whole.transpose(1, 0, 2, 3).reshape(2, feats, r)
    return whole[0], whole[1]


def body(adapter_input_weight, adapter_output_weight, initial_output_basis, initial_input_basis):
    tenants, rank, feats = adapter_output_weight.shape
    r = initial_output_basis.shape[1]
    n = lax.axis_size("feat")
    w_out = adapter_output_weight.reshape(tenants * rank, feats)
    w_in = adapter_input_weight.reshape(tenants * rank, feats)
    root = 1.0 / math.sqrt(PROJ_WIDTH)

    def projections(u, v):
        return [
            mm(w_out, u, 1, 0).reshape(n, rank, r),
            mm(w_in, v, 1, 0).reshape(n, rank, r),
        ]

    own = scatter_sum(jnp.concatenate(projections(initial_output_basis, initial_input_basis), 1), "feat")
    own = own * root
    p, q = own[:rank], own[rank:]
    f_out = mm(mm(q, q, 1, 1), p, 1, 0)
    f_in = mm(mm(p, p, 1, 1), q, 1, 0)
    factors = gather(jnp.concatenate([f_out, f_in], 0), "feat")
    f_out = factors[:, :rank].reshape(tenants * rank, r)
    f_in = factors[:, rank:].reshape(tenants * rank, r)

    for step in range(ITERS):
        u_new, v_new = update(w_out, w_in, f_out, f_in)
        grams = [
            mm(u_new, u_new, 0, 0).reshape(n, r // n, r),
            mm(v_new, v_new, 0, 0).reshape(n, r // n, r),
        ]
        own = scatter_sum(jnp.concatenate(projections(u_new, v_new) + grams, 1), "feat")
        last = step == ITERS - 1
        whole = gather(own[2 * rank:] if last else own, "feat")
        grams = whole if last else whole[:, 2 * rank:]
        half = r // n
        x_out = inverse_factor(grams[:, :half].reshape(r, r))
        x_in = inverse_factor(grams[:, half:].reshape(r, r))
        if not last:
            p = mm(whole[:, :rank].reshape(tenants * rank, r), x_out, 1, 1) * root
            q = mm(whole[:, rank:2 * rank].reshape(tenants * rank, r), x_in, 1, 1) * root
            p = p.reshape(tenants, rank, r)
            q = q.reshape(tenants, rank, r)
            f_out = bmm(bmm(q, q, 2, 2), p, 2, 1).reshape(tenants * rank, r)
            f_in = bmm(bmm(p, p, 2, 2), q, 2, 1).reshape(tenants * rank, r)
        else:
            p = mm(own[:rank], x_out, 1, 1) * root
            q = mm(own[rank:2 * rank], x_in, 1, 1) * root
            core = mm(p, q, 0, 0).reshape(n, r // n, r)
            cores = lax.all_to_all(core, "feat", 0, 0, tiled=True)
            u = mm(u_new, x_out, 1, 1)
            v = mm(v_new, x_in, 1, 1)
    return (cores, u, v)


def solution(mesh):
    placed = (
        P("tenant", None, "feat"),
        P("tenant", None, "feat"),
        P("feat", None),
        P("feat", None),
    )
    return jax.shard_map(
        body,
        mesh=mesh,
        in_specs=placed,
        out_specs=(P("tenant", "feat", None), P("feat", None), P("feat", None)),
        check_vma=False,
    )
```

```python
import functools
import math

import jax
import jax.numpy as jnp
from jax import lax
from jax.experimental import pallas as pl
from jax.experimental.pallas import tpu as pltpu
from jax.sharding import PartitionSpec as P

PROJ_WIDTH = 8192
ITERS = 2
HIGH_PRECISION = lax.Precision.HIGHEST
F32 = jnp.float32
BF16 = jnp.bfloat16
LANES = 128
PANEL = 8


def mm(a, b, ca, cb):
    return lax.dot_general(
        a, b, (((ca,), (cb,)), ((), ())), precision=HIGH_PRECISION, preferred_element_type=F32
    )


def bmm(a, b, ca, cb):
    return lax.dot_general(
        a, b, (((ca,), (cb,)), ((0,), (0,))), precision=HIGH_PRECISION, preferred_element_type=F32
    )


def split3(a):
    a1 = a.astype(BF16).astype(F32)
    rest = a - a1
    a2 = rest.astype(BF16).astype(F32)
    return a1, a2, rest - a2


def inverse_factor_kernel(gram_ref, x_ref):
    n = gram_ref.shape[-1]
    x_ref[...] = gram_ref[...] * (1.0 / PROJ_WIDTH)
    lane = lax.broadcasted_iota(jnp.int32, (PANEL, n), 1)
    sub = lax.broadcasted_iota(jnp.int32, (PANEL, n), 0)
    widen = lambda v: jnp.concatenate([v] * (n // LANES), 1)
    for k in range(0, n, PANEL):
        end = k + PANEL
        panel = x_ref[k:end, :]
        rows = [jnp.broadcast_to(panel[r:r + 1, :], (PANEL, n)) for r in range(PANEL)]
        d = [
            [jnp.broadcast_to(rows[r][:, k + c:k + c + 1], (PANEL, LANES)) if c >= r else None
             for c in range(PANEL)]
            for r in range(PANEL)
        ]
        inside = (lane >= k) & (lane < end)
        rows = [
            jnp.where(inside, jnp.where(lane == k + r, 1.0, 0.0), rows[r]) for r in range(PANEL)
        ]
        for j in range(PANEL):
            s = lax.rsqrt(d[j][j])
            rows[j] = rows[j] * widen(s)
            u = [d[j][c] * s if c > j else None for c in range(PANEL)]
            for r in range(j + 1, PANEL):
                for c in range(r, PANEL):
                    d[r][c] = d[r][c] - u[r] * u[c]
                rows[r] = rows[r] - widen(u[r]) * rows[j]
        new = rows[PANEL - 1]
        for r in range(PANEL - 2, -1, -1):
            new = jnp.where(sub == r, rows[r], new)
        x_ref[k:end, :] = new
        if end < n:
            lo = end // LANES * LANES
            a = split3(jnp.where(lane >= end, new, 0.0)[:, lo:])
            b = split3(new)
            lhs = jnp.concatenate([a[0], a[0], a[1], a[1], a[0], a[2]], 0).astype(BF16)
            rhs = jnp.concatenate([b[0], b[1], b[0], b[1], b[2], b[0]], 0).astype(BF16)
            change = lax.dot_general(
                lhs, rhs, (((0,), (0,)), ((), ())), preferred_element_type=F32
            )
            old = x_ref[end:, :]
            at = lax.broadcasted_iota(jnp.int32, old.shape, 1)
            old = jnp.where((at >= k) & (at < end), 0.0, old)
            x_ref[end:, :] = old - change[end - lo:, :]
    row = lax.broadcasted_iota(jnp.int32, (n, n), 0)
    col = lax.broadcasted_iota(jnp.int32, (n, n), 1)
    x_ref[...] = jnp.where(col <= row, x_ref[...], 0.0)


def inverse_factor(gram):
    return pl.pallas_call(
        inverse_factor_kernel,
        out_shape=jax.ShapeDtypeStruct(gram.shape, F32),
        in_specs=[pl.BlockSpec(memory_space=pltpu.VMEM)],
        out_specs=pl.BlockSpec(memory_space=pltpu.VMEM),
    )(gram)


def exchange(chunks, axis, groups):
    return lax.all_to_all(chunks, axis, 0, 0, tiled=True, axis_index_groups=groups)


def scatter_sum(chunks, axis, groups):
    return jnp.sum(exchange(chunks, axis, groups), axis=0)


def gather(own, axis, groups):
    return exchange(jnp.broadcast_to(own[None], (len(groups[0]),) + own.shape), axis, groups)


def body(adapter_input_weight, adapter_output_weight, initial_output_basis, initial_input_basis):
    tenants, rank, feats = adapter_output_weight.shape
    r = initial_output_basis.shape[1]
    n_feat, n_tenant = lax.axis_size("feat"), lax.axis_size("tenant")
    chips = n_feat // 2
    core = lax.axis_index("feat") % 2
    same_core = [[2 * i + c for i in range(chips)] for c in range(2)]
    n_z = n_tenant // 2
    along_z = [[h * n_z + z for z in range(n_z)] for h in range(2)]
    swap_cores = [(i, i ^ 1) for i in range(n_feat)]
    swap_halves = [(i, (i + n_z) % n_tenant) for i in range(n_tenant)]
    root = 1.0 / math.sqrt(PROJ_WIDTH)
    mine = tenants // chips

    def pick(for_out, for_in):
        return jnp.where(core == 0, for_out, for_in)

    def to_partner(x):
        return lax.ppermute(x, "feat", swap_cores)

    w_out = adapter_output_weight.reshape(tenants * rank, feats)
    w_in = adapter_input_weight.reshape(tenants * rank, feats)
    sent = pick(
        jnp.concatenate([w_in, initial_input_basis], 0),
        jnp.concatenate([w_out, initial_output_basis], 0),
    )
    got = to_partner(sent)
    w = jnp.concatenate([pick(w_out, w_in), got[:tenants * rank]], 1)
    basis = jnp.concatenate([pick(initial_output_basis, initial_input_basis), got[tenants * rank:]], 0)

    partial = mm(w, basis, 1, 0).reshape(chips, mine * rank, r)
    p = (scatter_sum(partial, "feat", same_core) * root).reshape(mine, rank, r)
    other_gram = to_partner(bmm(p, p, 2, 2))
    factor = gather(bmm(other_gram, p, 2, 1).reshape(mine * rank, r), "feat", same_core)
    factor = factor.reshape(tenants * rank, r)

    for step in range(ITERS):
        part = mm(w, factor, 0, 0).reshape(n_z, 2 * feats // n_z, r)
        own = scatter_sum(part, "tenant", along_z)
        own = own + lax.ppermute(own, "tenant", swap_halves)
        raw = gather(own, "tenant", along_z).reshape(2 * feats, r)
        partial = mm(w, raw, 1, 0).reshape(chips, mine * rank, r)
        gram = mm(raw, raw, 0, 0).reshape(chips, r // chips, r)
        own = scatter_sum(jnp.concatenate([partial, gram], 1), "feat", same_core)
        if step < ITERS - 1:
            whole = gather(own, "feat", same_core)
            x = inverse_factor(whole[:, mine * rank:].reshape(r, r))
            p = mm(whole[:, :mine * rank].reshape(tenants * rank, r), x, 1, 1) * root
            p = p.reshape(tenants, rank, r)
            other_gram = to_partner(bmm(p, p, 2, 2))
            factor = bmm(other_gram, p, 2, 1).reshape(tenants * rank, r)
        else:
            x = inverse_factor(gather(own[mine * rank:], "feat", same_core).reshape(r, r))
            p = (mm(own[:mine * rank], x, 1, 1) * root).reshape(mine, rank, r)
            other = to_partner(p)
            p_out, p_in = pick(p, other), pick(other, p)
            rows = p_out.reshape(mine, rank, chips, 2, r // n_feat)
            rows = pick(rows[:, :, :, 0], rows[:, :, :, 1]).reshape(mine, rank, r // 2)
            made = bmm(rows, p_in, 1, 1).reshape(mine, chips, r // n_feat, r)
            cores = exchange(made.transpose(1, 0, 2, 3), "feat", same_core)
            cores = cores.reshape(tenants, r // n_feat, r)
            away = to_partner(mm(raw[feats:], x, 1, 1))
            here = mm(raw[:feats], x, 1, 1)
    return cores, pick(here, away), pick(away, here)


def solution(mesh):
    placed = (
        P("tenant", None, "feat"),
        P("tenant", None, "feat"),
        P("feat", None),
        P("feat", None),
    )
    return jax.shard_map(
        body,
        mesh=mesh,
        in_specs=placed,
        out_specs=(P("tenant", "feat", None), P("feat", None), P("feat", None)),
        check_vma=False,
    )
```

```python
import functools
import math

import jax
import jax.numpy as jnp
from jax import lax
from jax.experimental import pallas as pl
from jax.experimental.pallas import tpu as pltpu
from jax.sharding import PartitionSpec as P

PROJ_WIDTH = 8192
ITERS = 2
HIGH_PRECISION = lax.Precision.HIGHEST
F32 = jnp.float32
BF16 = jnp.bfloat16
LANES = 128
PANEL = 8


def mm(a, b, ca, cb):
    return lax.dot_general(
        a, b, (((ca,), (cb,)), ((), ())), precision=HIGH_PRECISION, preferred_element_type=F32
    )


def bmm(a, b, ca, cb):
    return lax.dot_general(
        a, b, (((ca,), (cb,)), ((0,), (0,))), precision=HIGH_PRECISION, preferred_element_type=F32
    )


def split3(a):
    a1 = a.astype(BF16).astype(F32)
    rest = a - a1
    a2 = rest.astype(BF16).astype(F32)
    return a1, a2, rest - a2


def inverse_factor_kernel(gram_ref, x_ref):
    n = gram_ref.shape[-1]
    x_ref[...] = gram_ref[...] * (1.0 / PROJ_WIDTH)
    lane = lax.broadcasted_iota(jnp.int32, (PANEL, n), 1)
    sub = lax.broadcasted_iota(jnp.int32, (PANEL, n), 0)
    widen = lambda v: jnp.concatenate([v] * (n // LANES), 1)
    spread = lambda row, at: jnp.broadcast_to(row[:, at:at + 1], (PANEL, LANES))
    before = None
    for k in range(0, n, PANEL):
        end = k + PANEL
        panel = x_ref[k:end, :]
        rows = [jnp.broadcast_to(panel[r:r + 1, :], (PANEL, n)) for r in range(PANEL)]
        if before is not None:
            rows = [jnp.where((lane >= k - PANEL) & (lane < k), 0.0, row) for row in rows]
            for y in before:
                rows = [row - widen(spread(y, k + r)) * y for r, row in enumerate(rows)]
        d = [
            [spread(rows[r], k + c) if c >= r else None for c in range(PANEL)]
            for r in range(PANEL)
        ]
        inside = (lane >= k) & (lane < end)
        rows = [
            jnp.where(inside, jnp.where(lane == k + r, 1.0, 0.0), rows[r]) for r in range(PANEL)
        ]
        for j in range(PANEL):
            s = lax.rsqrt(d[j][j])
            rows[j] = rows[j] * widen(s)
            u = [d[j][c] * s if c > j else None for c in range(PANEL)]
            for r in range(j + 1, PANEL):
                for c in range(r, PANEL):
                    d[r][c] = d[r][c] - u[r] * u[c]
                rows[r] = rows[r] - widen(u[r]) * rows[j]
        new = rows[PANEL - 1]
        for r in range(PANEL - 2, -1, -1):
            new = jnp.where(sub == r, rows[r], new)
        x_ref[k:end, :] = new
        before = rows
        rest = end + PANEL
        if rest < n:
            lo = rest // LANES * LANES
            a = split3(jnp.where(lane >= rest, new, 0.0)[:, lo:])
            b = split3(new)
            lhs = jnp.concatenate([a[0], a[0], a[1], a[1], a[0], a[2]], 0).astype(BF16)
            rhs = jnp.concatenate([b[0], b[1], b[0], b[1], b[2], b[0]], 0).astype(BF16)
            change = lax.dot_general(
                lhs, rhs, (((0,), (0,)), ((), ())), preferred_element_type=F32
            )
            old = x_ref[rest:, :]
            at = lax.broadcasted_iota(jnp.int32, old.shape, 1)
            old = jnp.where((at >= k) & (at < end), 0.0, old)
            x_ref[rest:, :] = old - change[rest - lo:, :]
    row = lax.broadcasted_iota(jnp.int32, (n, n), 0)
    col = lax.broadcasted_iota(jnp.int32, (n, n), 1)
    x_ref[...] = jnp.where(col <= row, x_ref[...], 0.0)


def inverse_factor(gram):
    return pl.pallas_call(
        inverse_factor_kernel,
        out_shape=jax.ShapeDtypeStruct(gram.shape, F32),
        in_specs=[pl.BlockSpec(memory_space=pltpu.VMEM)],
        out_specs=pl.BlockSpec(memory_space=pltpu.VMEM),
    )(gram)


def exchange(chunks, axis, groups):
    return lax.all_to_all(chunks, axis, 0, 0, tiled=True, axis_index_groups=groups)


def scatter_sum(chunks, axis, groups):
    return jnp.sum(exchange(chunks, axis, groups), axis=0)


def gather(own, axis, groups):
    return exchange(jnp.broadcast_to(own[None], (len(groups[0]),) + own.shape), axis, groups)


def body(adapter_input_weight, adapter_output_weight, initial_output_basis, initial_input_basis):
    tenants, rank, feats = adapter_output_weight.shape
    r = initial_output_basis.shape[1]
    n_feat, n_tenant = lax.axis_size("feat"), lax.axis_size("tenant")
    chips = n_feat // 2
    core = lax.axis_index("feat") % 2
    same_core = [[2 * i + c for i in range(chips)] for c in range(2)]
    n_z = n_tenant // 2
    along_z = [[h * n_z + z for z in range(n_z)] for h in range(2)]
    swap_cores = [(i, i ^ 1) for i in range(n_feat)]
    swap_halves = [(i, (i + n_z) % n_tenant) for i in range(n_tenant)]
    root = 1.0 / math.sqrt(PROJ_WIDTH)
    mine = tenants // chips

    def pick(for_out, for_in):
        return jnp.where(core == 0, for_out, for_in)

    def to_partner(x):
        return lax.ppermute(x, "feat", swap_cores)

    w_out = adapter_output_weight.reshape(tenants * rank, feats)
    w_in = adapter_input_weight.reshape(tenants * rank, feats)
    sent = pick(
        jnp.concatenate([w_in, initial_input_basis], 0),
        jnp.concatenate([w_out, initial_output_basis], 0),
    )
    got = to_partner(sent)
    w = jnp.concatenate([pick(w_out, w_in), got[:tenants * rank]], 1)
    basis = jnp.concatenate([pick(initial_output_basis, initial_input_basis), got[tenants * rank:]], 0)

    partial = mm(w, basis, 1, 0).reshape(chips, mine * rank, r)
    p = (scatter_sum(partial, "feat", same_core) * root).reshape(mine, rank, r)
    other_gram = to_partner(bmm(p, p, 2, 2))
    factor = gather(bmm(other_gram, p, 2, 1).reshape(mine * rank, r), "feat", same_core)
    factor = factor.reshape(tenants * rank, r)

    for step in range(ITERS):
        part = mm(w, factor, 0, 0)
        own = scatter_sum(part.reshape(n_z, 2 * feats // n_z, r), "tenant", along_z)
        own = own + lax.ppermute(own, "tenant", swap_halves)
        raw = gather(own, "tenant", along_z).reshape(2 * feats, r)
        partial = mm(w, raw, 1, 0).reshape(chips, mine * rank, r)
        gram = mm(raw, raw, 0, 0).reshape(chips, r // chips, r)
        own = scatter_sum(jnp.concatenate([partial, gram], 1), "feat", same_core)
        whole = gather(own, "feat", same_core)
        x = inverse_factor(whole[:, mine * rank:].reshape(r, r))
        p = mm(whole[:, :mine * rank].reshape(tenants * rank, r), x, 1, 1) * root
        if step < ITERS - 1:
            p = p.reshape(tenants, rank, r)
            other_gram = to_partner(bmm(p, p, 2, 2))
            factor = bmm(other_gram, p, 2, 1).reshape(tenants * rank, r)
    other = to_partner(p)
    away = to_partner(mm(raw[feats:], x, 1, 1))
    here = mm(raw[:feats], x, 1, 1)
    n_rows = r // n_feat
    first = lax.axis_index("feat") * n_rows
    one_hot = lax.broadcasted_iota(jnp.int32, (n_rows, r), 1) == (
        first + lax.broadcasted_iota(jnp.int32, (n_rows, r), 0)
    )
    cols = mm(one_hot.astype(F32), pick(p, other), 1, 1)
    shape = (tenants, n_rows, tenants * rank)
    own_tenant = lax.broadcasted_iota(jnp.int32, shape, 2) // rank == lax.broadcasted_iota(
        jnp.int32, shape, 0
    )
    blocks = jnp.where(own_tenant, cols[None], 0.0).reshape(tenants * n_rows, tenants * rank)
    cores = mm(blocks, pick(other, p), 1, 0).reshape(tenants, n_rows, r)
    return cores, pick(here, away), pick(away, here)


def solution(mesh):
    placed = (
        P("tenant", None, "feat"),
        P("tenant", None, "feat"),
        P("feat", None),
        P("feat", None),
    )
    return jax.shard_map(
        body,
        mesh=mesh,
        in_specs=placed,
        out_specs=(P("tenant", "feat", None), P("feat", None), P("feat", None)),
        check_vma=False,
    )
```

```python
import functools
import math

import jax
import jax.numpy as jnp
from jax import lax
from jax.experimental import pallas as pl
from jax.experimental.pallas import tpu as pltpu
from jax.sharding import PartitionSpec as P

PROJ_WIDTH = 8192
ITERS = 2
HIGH_PRECISION = lax.Precision.HIGHEST
F32 = jnp.float32
BF16 = jnp.bfloat16
LANES = 128
PANEL = 8
VMEM_BYTES = 32 * 1024 * 1024


def mm(a, b, ca, cb):
    return lax.dot_general(
        a, b, (((ca,), (cb,)), ((), ())), precision=HIGH_PRECISION, preferred_element_type=F32
    )


def bmm(a, b, ca, cb):
    return lax.dot_general(
        a, b, (((ca,), (cb,)), ((0,), (0,))), precision=HIGH_PRECISION, preferred_element_type=F32
    )


def split3(a):
    a1 = a.astype(BF16).astype(F32)
    rest = a - a1
    a2 = rest.astype(BF16).astype(F32)
    return a1, a2, rest - a2


def invert_factor(x_ref):
    n = x_ref.shape[-1]
    lane = lax.broadcasted_iota(jnp.int32, (PANEL, n), 1)
    sub = lax.broadcasted_iota(jnp.int32, (PANEL, n), 0)
    widen = lambda v: jnp.concatenate([v] * (n // LANES), 1)
    spread = lambda row, at: jnp.broadcast_to(row[:, at:at + 1], (PANEL, LANES))
    before = None
    for k in range(0, n, PANEL):
        end = k + PANEL
        panel = x_ref[k:end, :]
        rows = [jnp.broadcast_to(panel[r:r + 1, :], (PANEL, n)) for r in range(PANEL)]
        if before is not None:
            rows = [jnp.where((lane >= k - PANEL) & (lane < k), 0.0, row) for row in rows]
            for y in before:
                rows = [row - widen(spread(y, k + r)) * y for r, row in enumerate(rows)]
        d = [
            [spread(rows[r], k + c) if c >= r else None for c in range(PANEL)]
            for r in range(PANEL)
        ]
        inside = (lane >= k) & (lane < end)
        rows = [
            jnp.where(inside, jnp.where(lane == k + r, 1.0, 0.0), rows[r]) for r in range(PANEL)
        ]
        for j in range(PANEL):
            s = lax.rsqrt(d[j][j])
            rows[j] = rows[j] * widen(s)
            u = [d[j][c] * s if c > j else None for c in range(PANEL)]
            for r in range(j + 1, PANEL):
                for c in range(r, PANEL):
                    d[r][c] = d[r][c] - u[r] * u[c]
                rows[r] = rows[r] - widen(u[r]) * rows[j]
        new = rows[PANEL - 1]
        for r in range(PANEL - 2, -1, -1):
            new = jnp.where(sub == r, rows[r], new)
        x_ref[k:end, :] = new
        before = rows
        rest = end + PANEL
        if rest < n:
            lo = rest // LANES * LANES
            a = split3(jnp.where(lane >= rest, new, 0.0)[:, lo:])
            b = split3(new)
            lhs = jnp.concatenate([a[0], a[0], a[1], a[1], a[0], a[2]], 0).astype(BF16)
            rhs = jnp.concatenate([b[0], b[1], b[0], b[1], b[2], b[0]], 0).astype(BF16)
            change = lax.dot_general(
                lhs, rhs, (((0,), (0,)), ((), ())), preferred_element_type=F32
            )
            old = x_ref[rest:, :]
            at = lax.broadcasted_iota(jnp.int32, old.shape, 1)
            old = jnp.where((at >= k) & (at < end), 0.0, old)
            x_ref[rest:, :] = old - change[rest - lo:, :]
    row = lax.broadcasted_iota(jnp.int32, (n, n), 0)
    col = lax.broadcasted_iota(jnp.int32, (n, n), 1)
    x_ref[...] = jnp.where(col <= row, x_ref[...], 0.0)


def project_kernel(w_ref, raw_ref, out_ref):
    chips = out_ref.shape[0]
    rows = w_ref.shape[0] // chips
    raw = raw_ref[...]
    y = mm(w_ref[...], raw, 1, 0)
    for i in range(chips):
        for h in range(2):
            out_ref[i, h * rows:(h + 1) * rows, :] = (
                y[i * rows:(i + 1) * rows, h * LANES:(h + 1) * LANES]
            )
    top = mm(raw[:, :LANES], raw, 0, 0)
    low = mm(raw[:, LANES:], raw[:, LANES:], 0, 0)
    per_chip = 3 * LANES // chips
    for j, block in enumerate((top[:, :LANES], top[:, LANES:], low)):
        for k in range(0, LANES, 8):
            at = j * LANES + k
            i, off = at // per_chip, at % per_chip + 2 * rows
            out_ref[i, off:off + 8, :] = block[k:k + 8, :]


def project(w, raw, chips):
    rows = 2 * w.shape[0] // chips + 3 * LANES // chips
    return pl.pallas_call(
        project_kernel,
        out_shape=jax.ShapeDtypeStruct((chips, rows, LANES), F32),
        in_specs=[pl.BlockSpec(memory_space=pltpu.VMEM)] * 2,
        out_specs=pl.BlockSpec(memory_space=pltpu.VMEM),
        compiler_params=pltpu.CompilerParams(vmem_limit_bytes=VMEM_BYTES),
    )(w, raw)


def factor_and_project(whole_ref, x_ref, y_ref):
    chips = whole_ref.shape[0]
    rows = y_ref.shape[0] // chips
    per_chip = 3 * LANES // chips
    for i in range(chips):
        for h in range(2):
            y_ref[i * rows:(i + 1) * rows, h * LANES:(h + 1) * LANES] = (
                whole_ref[i, h * rows:(h + 1) * rows, :]
            )
    x_ref[LANES:, :LANES] = jnp.zeros((LANES, LANES), F32)
    for j, (top, left) in enumerate(((0, 0), (0, LANES), (LANES, LANES))):
        for k in range(0, LANES, 8):
            at = j * LANES + k
            i, off = at // per_chip, at % per_chip + 2 * rows
            x_ref[top + k:top + k + 8, left:left + LANES] = (
                whole_ref[i, off:off + 8, :] * (1.0 / PROJ_WIDTH)
            )
    invert_factor(x_ref)
    return mm(y_ref[...], x_ref[...], 1, 1) * (1.0 / math.sqrt(PROJ_WIDTH))


def middle_kernel(whole_ref, p_ref, x_ref, y_ref):
    p_ref[...] = factor_and_project(whole_ref, x_ref, y_ref)


def last_kernel(whole_ref, raw_ref, sent_ref, here_ref, x_ref, y_ref):
    n = y_ref.shape[0]
    half = here_ref.shape[0]
    sent_ref[:n, :] = factor_and_project(whole_ref, x_ref, y_ref)
    basis = mm(raw_ref[...], x_ref[...], 1, 1)
    here_ref[...] = basis[:half, :]
    sent_ref[n:, :] = basis[half:, :]


def call_on_whole(kernel, outs, n, r, *args):
    return pl.pallas_call(
        kernel,
        out_shape=[jax.ShapeDtypeStruct((rows, r), F32) for rows in outs],
        in_specs=[pl.BlockSpec(memory_space=pltpu.VMEM)] * len(args),
        out_specs=[pl.BlockSpec(memory_space=pltpu.VMEM)] * len(outs),
        scratch_shapes=[pltpu.VMEM((r, r), F32), pltpu.VMEM((n, r), F32)],
        compiler_params=pltpu.CompilerParams(vmem_limit_bytes=VMEM_BYTES),
    )(*args)


def exchange(chunks, axis, groups):
    return lax.all_to_all(chunks, axis, 0, 0, tiled=True, axis_index_groups=groups)


def scatter_sum(chunks, axis, groups):
    return jnp.sum(exchange(chunks, axis, groups), axis=0)


def gather(own, axis, groups):
    return exchange(jnp.broadcast_to(own[None], (len(groups[0]),) + own.shape), axis, groups)


def body(adapter_input_weight, adapter_output_weight, initial_output_basis, initial_input_basis):
    tenants, rank, feats = adapter_output_weight.shape
    r = initial_output_basis.shape[1]
    n_feat, n_tenant = lax.axis_size("feat"), lax.axis_size("tenant")
    chips = n_feat // 2
    core = lax.axis_index("feat") % 2
    same_core = [[2 * i + c for i in range(chips)] for c in range(2)]
    n_z = n_tenant // 2
    along_z = [[h * n_z + z for z in range(n_z)] for h in range(2)]
    swap_cores = [(i, i ^ 1) for i in range(n_feat)]
    swap_halves = [(i, (i + n_z) % n_tenant) for i in range(n_tenant)]
    root = 1.0 / math.sqrt(PROJ_WIDTH)
    mine = tenants // chips

    def pick(for_out, for_in):
        return jnp.where(core == 0, for_out, for_in)

    def to_partner(x):
        return lax.ppermute(x, "feat", swap_cores)

    w_out = adapter_output_weight.reshape(tenants * rank, feats)
    w_in = adapter_input_weight.reshape(tenants * rank, feats)
    sent = pick(
        jnp.concatenate([w_in, initial_input_basis], 0),
        jnp.concatenate([w_out, initial_output_basis], 0),
    )
    got = to_partner(sent)
    w = jnp.concatenate([pick(w_out, w_in), got[:tenants * rank]], 1)
    basis = jnp.concatenate([pick(initial_output_basis, initial_input_basis), got[tenants * rank:]], 0)

    partial = mm(w, basis, 1, 0).reshape(chips, mine * rank, r)
    p = (scatter_sum(partial, "feat", same_core) * root).reshape(mine, rank, r)
    other_gram = to_partner(bmm(p, p, 2, 2))
    factor = gather(bmm(other_gram, p, 2, 1).reshape(mine * rank, r), "feat", same_core)
    factor = factor.reshape(tenants * rank, r)

    for step in range(ITERS):
        part = mm(w, factor, 0, 0)
        own = scatter_sum(part.reshape(n_z, 2 * feats // n_z, r), "tenant", along_z)
        own = own + lax.ppermute(own, "tenant", swap_halves)
        raw = gather(own, "tenant", along_z).reshape(2 * feats, r)
        own = scatter_sum(project(w, raw, chips), "feat", same_core)
        whole = gather(own, "feat", same_core)
        n = tenants * rank
        if step < ITERS - 1:
            p = call_on_whole(middle_kernel, [n], n, r, whole)[0].reshape(tenants, rank, r)
            other_gram = to_partner(bmm(p, p, 2, 2))
            factor = bmm(other_gram, p, 2, 1).reshape(n, r)
    sent, here = call_on_whole(last_kernel, [n + feats, feats], n, r, whole, raw)
    got = to_partner(sent)
    p, other, away = sent[:n], got[:n], got[n:]
    n_rows = r // n_feat
    first = lax.axis_index("feat") * n_rows
    one_hot = lax.broadcasted_iota(jnp.int32, (n_rows, r), 1) == (
        first + lax.broadcasted_iota(jnp.int32, (n_rows, r), 0)
    )
    cols = mm(one_hot.astype(F32), pick(p, other), 1, 1)
    shape = (tenants, n_rows, tenants * rank)
    own_tenant = lax.broadcasted_iota(jnp.int32, shape, 2) // rank == lax.broadcasted_iota(
        jnp.int32, shape, 0
    )
    blocks = jnp.where(own_tenant, cols[None], 0.0).reshape(tenants * n_rows, tenants * rank)
    cores = mm(blocks, pick(other, p), 1, 0).reshape(tenants, n_rows, r)
    return cores, pick(here, away), pick(away, here)


def solution(mesh):
    placed = (
        P("tenant", None, "feat"),
        P("tenant", None, "feat"),
        P("feat", None),
        P("feat", None),
    )
    return jax.shard_map(
        body,
        mesh=mesh,
        in_specs=placed,
        out_specs=(P("tenant", "feat", None), P("feat", None), P("feat", None)),
        check_vma=False,
    )
```

```python
import functools
import math

import jax
import jax.numpy as jnp
from jax import lax
from jax.experimental import pallas as pl
from jax.experimental.pallas import tpu as pltpu
from jax.sharding import PartitionSpec as P

PROJ_WIDTH = 8192
ITERS = 2
HIGH_PRECISION = lax.Precision.HIGHEST
F32 = jnp.float32
BF16 = jnp.bfloat16
LANES = 128
PANEL = 8
VMEM_BYTES = 32 * 1024 * 1024


def mm(a, b, ca, cb):
    return lax.dot_general(
        a, b, (((ca,), (cb,)), ((), ())), precision=HIGH_PRECISION, preferred_element_type=F32
    )


def split3(a):
    a1 = a.astype(BF16).astype(F32)
    rest = a - a1
    a2 = rest.astype(BF16).astype(F32)
    return a1, a2, rest - a2


def invert_factor(x_ref):
    n = x_ref.shape[-1]
    lane = lax.broadcasted_iota(jnp.int32, (PANEL, n), 1)
    sub = lax.broadcasted_iota(jnp.int32, (PANEL, n), 0)
    widen = lambda v: jnp.concatenate([v] * (n // LANES), 1)
    spread = lambda row, at: jnp.broadcast_to(row[:, at:at + 1], (PANEL, LANES))
    before = None
    for k in range(0, n, PANEL):
        end = k + PANEL
        panel = x_ref[k:end, :]
        rows = [jnp.broadcast_to(panel[r:r + 1, :], (PANEL, n)) for r in range(PANEL)]
        if before is not None:
            rows = [jnp.where((lane >= k - PANEL) & (lane < k), 0.0, row) for row in rows]
            for y in before:
                rows = [row - widen(spread(y, k + r)) * y for r, row in enumerate(rows)]
        d = [
            [spread(rows[r], k + c) if c >= r else None for c in range(PANEL)]
            for r in range(PANEL)
        ]
        inside = (lane >= k) & (lane < end)
        rows = [
            jnp.where(inside, jnp.where(lane == k + r, 1.0, 0.0), rows[r]) for r in range(PANEL)
        ]
        for j in range(PANEL):
            s = lax.rsqrt(d[j][j])
            rows[j] = rows[j] * widen(s)
            u = [d[j][c] * s if c > j else None for c in range(PANEL)]
            for r in range(j + 1, PANEL):
                for c in range(r, PANEL):
                    d[r][c] = d[r][c] - u[r] * u[c]
                rows[r] = rows[r] - widen(u[r]) * rows[j]
        new = rows[PANEL - 1]
        for r in range(PANEL - 2, -1, -1):
            new = jnp.where(sub == r, rows[r], new)
        x_ref[k:end, :] = new
        before = rows
        rest = end + PANEL
        if rest < n:
            lo = rest // LANES * LANES
            a = split3(jnp.where(lane >= rest, new, 0.0)[:, lo:])
            b = split3(new)
            lhs = jnp.concatenate([a[0], a[0], a[1], a[1], a[0], a[2]], 0).astype(BF16)
            rhs = jnp.concatenate([b[0], b[1], b[0], b[1], b[2], b[0]], 0).astype(BF16)
            change = lax.dot_general(
                lhs, rhs, (((0,), (0,)), ((), ())), preferred_element_type=F32
            )
            old = x_ref[rest:, :]
            at = lax.broadcasted_iota(jnp.int32, old.shape, 1)
            old = jnp.where((at >= k) & (at < end), 0.0, old)
            x_ref[rest:, :] = old - change[rest - lo:, :]
    row = lax.broadcasted_iota(jnp.int32, (n, n), 0)
    col = lax.broadcasted_iota(jnp.int32, (n, n), 1)
    x_ref[...] = jnp.where(col <= row, x_ref[...], 0.0)


def project_kernel(w_ref, raw_ref, out_ref):
    chips = out_ref.shape[0]
    side = math.isqrt(chips)
    chip_of = lambda b: b % side * side + b // side
    rows = w_ref.shape[0] // chips
    raw = raw_ref[...]
    y = mm(w_ref[...], raw, 1, 0)
    for i in range(chips):
        for h in range(2):
            out_ref[chip_of(i), h * rows:(h + 1) * rows, :] = (
                y[i * rows:(i + 1) * rows, h * LANES:(h + 1) * LANES]
            )
    top = mm(raw[:, :LANES], raw, 0, 0)
    low = mm(raw[:, LANES:], raw[:, LANES:], 0, 0)
    per_chip = 3 * LANES // chips
    for j, block in enumerate((top[:, :LANES], top[:, LANES:], low)):
        for k in range(0, LANES, 8):
            at = j * LANES + k
            i, off = at // per_chip, at % per_chip + 2 * rows
            out_ref[chip_of(i), off:off + 8, :] = block[k:k + 8, :]


def factor_and_project(whole_ref, x_ref, y_ref):
    chips = whole_ref.shape[0]
    rows = y_ref.shape[0] // chips
    per_chip = 3 * LANES // chips
    for i in range(chips):
        for h in range(2):
            y_ref[i * rows:(i + 1) * rows, h * LANES:(h + 1) * LANES] = (
                whole_ref[i, h * rows:(h + 1) * rows, :]
            )
    x_ref[LANES:, :LANES] = jnp.zeros((LANES, LANES), F32)
    for j, (top, left) in enumerate(((0, 0), (0, LANES), (LANES, LANES))):
        for k in range(0, LANES, 8):
            at = j * LANES + k
            i, off = at // per_chip, at % per_chip + 2 * rows
            x_ref[top + k:top + k + 8, left:left + LANES] = (
                whole_ref[i, off:off + 8, :] * (1.0 / PROJ_WIDTH)
            )
    invert_factor(x_ref)
    return mm(y_ref[...], x_ref[...], 1, 1) * (1.0 / math.sqrt(PROJ_WIDTH))


def same_block(shape, row_block, col_block):
    return (
        lax.broadcasted_iota(jnp.int32, shape, 0) // row_block
        == lax.broadcasted_iota(jnp.int32, shape, 1) // col_block
    )


def first_gram_kernel(rank, parts_ref, p_ref, gram_ref):
    p = jnp.sum(parts_ref[...], 0) * (1.0 / math.sqrt(PROJ_WIDTH))
    p_ref[...] = p
    gram = mm(p, p, 1, 1)
    gram_ref[...] = jnp.where(same_block(gram.shape, rank, rank), gram, 0.0)


def first_factor_kernel(p_ref, gram_ref, out_ref):
    factor = mm(gram_ref[...], p_ref[...], 1, 0)
    for i in range(out_ref.shape[0]):
        out_ref[i] = factor


def middle_kernel(rank, whole_ref, p_ref, gram_ref, x_ref, y_ref):
    p = factor_and_project(whole_ref, x_ref, y_ref)
    p_ref[...] = p
    for k in range(0, p.shape[0], LANES):
        gram = mm(p[k:k + LANES], p[k:k + LANES], 1, 1)
        gram = jnp.where(same_block(gram.shape, rank, rank), gram, 0.0)
        packed = gram[:rank]
        for i in range(rank, LANES, rank):
            packed = packed + gram[i:i + rank]
        gram_ref[:, k:k + LANES] = packed


def first_update_kernel(w_ref, factor_ref, part_ref):
    part_ref[...] = mm(w_ref[...], factor_ref[...], 0, 0)


def update_kernel(gram_ref, p_ref, w_ref, part_ref, f_ref):
    rank = gram_ref.shape[0]
    for k in range(0, f_ref.shape[0], LANES):
        gram = jnp.concatenate([gram_ref[:, k:k + LANES]] * (LANES // rank), 0)
        gram = jnp.where(same_block(gram.shape, rank, rank), gram, 0.0)
        f_ref[k:k + LANES, :] = mm(gram, p_ref[k:k + LANES, :], 1, 0)
    part_ref[...] = mm(w_ref[...], f_ref[...], 0, 0)


def cores_kernel(rank, n_rows, at_ref, sent_ref, got_ref, here_ref, cores_ref, out_ref, in_ref):
    n = sent_ref.shape[0] - here_ref.shape[0]
    r = here_ref.shape[1]
    at = at_ref[0]

    def place(mine, p_ref, q_ref):
        one_hot = lax.broadcasted_iota(jnp.int32, (n_rows, r), 1) == (
            at * n_rows + lax.broadcasted_iota(jnp.int32, (n_rows, r), 0)
        )
        cols = mm(one_hot.astype(F32), p_ref[:n, :], 1, 1)
        group = LANES // rank
        size = group * n_rows
        for i, k in enumerate(range(0, n, LANES)):
            block = jnp.concatenate([cols[:, k:k + LANES]] * group, 0)
            block = jnp.where(same_block(block.shape, n_rows, rank), block, 0.0)
            cores_ref[i * size:(i + 1) * size, :] = mm(block, q_ref[k:k + LANES, :], 1, 0)
        here, away = (out_ref, in_ref) if mine else (in_ref, out_ref)
        here[...] = here_ref[...]
        away[...] = got_ref[n:, :]

    @pl.when(at % 2 == 0)
    def _():
        place(True, sent_ref, got_ref)

    @pl.when(at % 2 == 1)
    def _():
        place(False, got_ref, sent_ref)


def last_kernel(whole_ref, raw_ref, sent_ref, here_ref, x_ref, y_ref):
    n = y_ref.shape[0]
    half = here_ref.shape[0]
    sent_ref[:n, :] = factor_and_project(whole_ref, x_ref, y_ref)
    basis = mm(raw_ref[...], x_ref[...], 1, 1)
    here_ref[...] = basis[:half, :]
    sent_ref[n:, :] = basis[half:, :]


def call(kernel, shapes, args, scratch=(), scalars=0):
    return pl.pallas_call(
        kernel,
        out_shape=[jax.ShapeDtypeStruct(shape, F32) for shape in shapes],
        in_specs=[pl.BlockSpec(memory_space=pltpu.SMEM)] * scalars
        + [pl.BlockSpec(memory_space=pltpu.VMEM)] * (len(args) - scalars),
        out_specs=[pl.BlockSpec(memory_space=pltpu.VMEM)] * len(shapes),
        scratch_shapes=[pltpu.VMEM(shape, F32) for shape in scratch],
        compiler_params=pltpu.CompilerParams(vmem_limit_bytes=VMEM_BYTES),
    )(*args)


def exchange(chunks, axis, groups):
    return lax.all_to_all(chunks, axis, 0, 0, tiled=True, axis_index_groups=groups)


def scatter_sum(chunks, axis, groups):
    return jnp.sum(exchange(chunks, axis, groups), axis=0)


def gather(own, axis, groups):
    return exchange(jnp.broadcast_to(own[None], (len(groups[0]),) + own.shape), axis, groups)


def body(adapter_input_weight, adapter_output_weight, initial_output_basis, initial_input_basis):
    tenants, rank, feats = adapter_output_weight.shape
    r = initial_output_basis.shape[1]
    n_feat, n_tenant = lax.axis_size("feat"), lax.axis_size("tenant")
    chips = n_feat // 2
    core = lax.axis_index("feat") % 2
    same_core = [[2 * i + c for i in range(chips)] for c in range(2)]
    side = math.isqrt(chips)
    along_x = [[(y * side + x) * 2 + c for x in range(side)] for y in range(side) for c in range(2)]
    along_y = [[(y * side + x) * 2 + c for y in range(side)] for x in range(side) for c in range(2)]
    n_z = n_tenant // 2
    along_z = [[h * n_z + z for z in range(n_z)] for h in range(2)]
    swap_cores = [(i, i ^ 1) for i in range(n_feat)]
    swap_halves = [(i, (i + n_z) % n_tenant) for i in range(n_tenant)]
    mine = tenants // chips

    def pick(for_out, for_in):
        return jnp.where(core == 0, for_out, for_in)

    def to_partner(x):
        return lax.ppermute(x, "feat", swap_cores)

    w_out = adapter_output_weight.reshape(tenants * rank, feats)
    w_in = adapter_input_weight.reshape(tenants * rank, feats)
    sent = pick(
        jnp.concatenate([w_in, initial_input_basis], 0),
        jnp.concatenate([w_out, initial_output_basis], 0),
    )
    got = to_partner(sent)
    w = jnp.concatenate([pick(w_out, w_in), got[:tenants * rank]], 1)
    basis = jnp.concatenate([pick(initial_output_basis, initial_input_basis), got[tenants * rank:]], 0)

    n = tenants * rank
    own_rows = mine * rank

    partial = mm(w, basis, 1, 0).reshape(chips, own_rows, r)
    p, gram = call(
        functools.partial(first_gram_kernel, rank),
        [(own_rows, r), (own_rows, own_rows)],
        [exchange(partial, "feat", same_core)],
    )
    copies = call(first_factor_kernel, [(chips, own_rows, r)], [p, to_partner(gram)])[0]
    factor = exchange(copies, "feat", same_core).reshape(n, r)
    part = call(first_update_kernel, [(2 * feats, r)], [w, factor])[0]

    for step in range(ITERS):
        own = scatter_sum(part.reshape(n_z, 2 * feats // n_z, r), "tenant", along_z)
        own = own + lax.ppermute(own, "tenant", swap_halves)
        raw = gather(own, "tenant", along_z).reshape(2 * feats, r)
        chunk = (chips, 2 * own_rows + 3 * LANES // chips, LANES)
        own = scatter_sum(call(project_kernel, [chunk], [w, raw])[0], "feat", same_core)
        whole = gather(gather(own, "feat", along_y), "feat", along_x).reshape(chunk)
        scratch = [(r, r), (n, r)]
        if step < ITERS - 1:
            p, gram = call(
                functools.partial(middle_kernel, rank), [(n, r), (rank, n)], [whole], scratch
            )
            part = call(update_kernel, [(2 * feats, r)], [to_partner(gram), p, w], [(n, r)])[0]
    sent, here = call(last_kernel, [(n + feats, r), (feats, r)], [whole, raw], scratch)
    n_rows = r // n_feat
    cores, out_basis, in_basis = call(
        functools.partial(cores_kernel, rank, n_rows),
        [(tenants * n_rows, r), (feats, r), (feats, r)],
        [lax.axis_index("feat").reshape(1), sent, to_partner(sent), here],
        scalars=1,
    )
    return cores.reshape(tenants, n_rows, r), out_basis, in_basis


def solution(mesh):
    placed = (
        P("tenant", None, "feat"),
        P("tenant", None, "feat"),
        P("feat", None),
        P("feat", None),
    )
    return jax.shard_map(
        body,
        mesh=mesh,
        in_specs=placed,
        out_specs=(P("tenant", "feat", None), P("feat", None), P("feat", None)),
        check_vma=False,
    )
```

```python
import functools
import math

import jax
import jax.numpy as jnp
from jax import lax
from jax.experimental import pallas as pl
from jax.experimental.pallas import tpu as pltpu
from jax.sharding import PartitionSpec as P

PROJ_WIDTH = 8192
ITERS = 2
HIGH_PRECISION = lax.Precision.HIGHEST
F32 = jnp.float32
BF16 = jnp.bfloat16
LANES = 128
PANEL = 8
VMEM_BYTES = 32 * 1024 * 1024


def mm(a, b, ca, cb):
    return lax.dot_general(
        a, b, (((ca,), (cb,)), ((), ())), precision=HIGH_PRECISION, preferred_element_type=F32
    )


def split3(a):
    a1 = a.astype(BF16).astype(F32)
    rest = a - a1
    a2 = rest.astype(BF16).astype(F32)
    return a1, a2, rest - a2


def invert_factor(x_ref):
    n = x_ref.shape[-1]
    lane = lax.broadcasted_iota(jnp.int32, (PANEL, n), 1)
    sub = lax.broadcasted_iota(jnp.int32, (PANEL, n), 0)
    widen = lambda v: jnp.concatenate([v] * (n // LANES), 1)
    spread = lambda row, at: jnp.broadcast_to(row[:, at:at + 1], (PANEL, LANES))
    before = None
    for k in range(0, n, PANEL):
        end = k + PANEL
        panel = x_ref[k:end, :]
        rows = [jnp.broadcast_to(panel[r:r + 1, :], (PANEL, n)) for r in range(PANEL)]
        if before is not None:
            rows = [jnp.where((lane >= k - PANEL) & (lane < k), 0.0, row) for row in rows]
            for y in before:
                rows = [row - widen(spread(y, k + r)) * y for r, row in enumerate(rows)]
        d = [
            [spread(rows[r], k + c) if c >= r else None for c in range(PANEL)]
            for r in range(PANEL)
        ]
        inside = (lane >= k) & (lane < end)
        rows = [
            jnp.where(inside, jnp.where(lane == k + r, 1.0, 0.0), rows[r]) for r in range(PANEL)
        ]
        for j in range(PANEL):
            s = lax.rsqrt(d[j][j])
            rows[j] = rows[j] * widen(s)
            u = [d[j][c] * s if c > j else None for c in range(PANEL)]
            for r in range(j + 1, PANEL):
                for c in range(r, PANEL):
                    d[r][c] = d[r][c] - u[r] * u[c]
                rows[r] = rows[r] - widen(u[r]) * rows[j]
        new = rows[PANEL - 1]
        for r in range(PANEL - 2, -1, -1):
            new = jnp.where(sub == r, rows[r], new)
        x_ref[k:end, :] = new
        before = rows
        rest = end + PANEL
        if rest < n:
            lo = rest // LANES * LANES
            a = split3(jnp.where(lane >= rest, new, 0.0)[:, lo:])
            b = split3(new)
            lhs = jnp.concatenate([a[0], a[0], a[1], a[1], a[0], a[2]], 0).astype(BF16)
            rhs = jnp.concatenate([b[0], b[1], b[0], b[1], b[2], b[0]], 0).astype(BF16)
            change = lax.dot_general(
                lhs, rhs, (((0,), (0,)), ((), ())), preferred_element_type=F32
            )
            old = x_ref[rest:, :]
            at = lax.broadcasted_iota(jnp.int32, old.shape, 1)
            old = jnp.where((at >= k) & (at < end), 0.0, old)
            x_ref[rest:, :] = old - change[rest - lo:, :]
    row = lax.broadcasted_iota(jnp.int32, (n, n), 0)
    col = lax.broadcasted_iota(jnp.int32, (n, n), 1)
    x_ref[...] = jnp.where(col <= row, x_ref[...], 0.0)


def project_kernel(w_ref, raw_ref, out_ref):
    chips = out_ref.shape[0]
    side = math.isqrt(chips)
    chip_of = lambda b: b % side * side + b // side
    rows = w_ref.shape[0] // chips
    raw = raw_ref[...]
    y = mm(w_ref[...], raw, 1, 0)
    for i in range(chips):
        for h in range(2):
            out_ref[chip_of(i), h * rows:(h + 1) * rows, :] = (
                y[i * rows:(i + 1) * rows, h * LANES:(h + 1) * LANES]
            )
    top = mm(raw[:, :LANES], raw, 0, 0)
    low = mm(raw[:, LANES:], raw[:, LANES:], 0, 0)
    per_chip = 3 * LANES // chips
    for j, block in enumerate((top[:, :LANES], top[:, LANES:], low)):
        for k in range(0, LANES, 8):
            at = j * LANES + k
            i, off = at // per_chip, at % per_chip + 2 * rows
            out_ref[chip_of(i), off:off + 8, :] = block[k:k + 8, :]


def factor_and_project(whole_ref, x_ref, y_ref):
    chips = whole_ref.shape[0]
    rows = y_ref.shape[0] // chips
    per_chip = 3 * LANES // chips
    for i in range(chips):
        for h in range(2):
            y_ref[i * rows:(i + 1) * rows, h * LANES:(h + 1) * LANES] = (
                whole_ref[i, h * rows:(h + 1) * rows, :]
            )
    x_ref[LANES:, :LANES] = jnp.zeros((LANES, LANES), F32)
    for j, (top, left) in enumerate(((0, 0), (0, LANES), (LANES, LANES))):
        for k in range(0, LANES, 8):
            at = j * LANES + k
            i, off = at // per_chip, at % per_chip + 2 * rows
            x_ref[top + k:top + k + 8, left:left + LANES] = (
                whole_ref[i, off:off + 8, :] * (1.0 / PROJ_WIDTH)
            )
    invert_factor(x_ref)
    return mm(y_ref[...], x_ref[...], 1, 1) * (1.0 / math.sqrt(PROJ_WIDTH))


def same_block(shape, row_block, col_block):
    return (
        lax.broadcasted_iota(jnp.int32, shape, 0) // row_block
        == lax.broadcasted_iota(jnp.int32, shape, 1) // col_block
    )


def first_gram_kernel(rank, parts_ref, p_ref, gram_ref):
    p = jnp.sum(parts_ref[...], 0) * (1.0 / math.sqrt(PROJ_WIDTH))
    p_ref[...] = p
    gram = mm(p, p, 1, 1)
    gram_ref[...] = jnp.where(same_block(gram.shape, rank, rank), gram, 0.0)


def first_factor_kernel(p_ref, gram_ref, out_ref):
    factor = mm(gram_ref[...], p_ref[...], 1, 0)
    for i in range(out_ref.shape[0]):
        out_ref[i] = factor


def middle_kernel(rank, whole_ref, p_ref, gram_ref, x_ref, y_ref):
    p = factor_and_project(whole_ref, x_ref, y_ref)
    p_ref[...] = p
    for k in range(0, p.shape[0], LANES):
        gram = mm(p[k:k + LANES], p[k:k + LANES], 1, 1)
        gram = jnp.where(same_block(gram.shape, rank, rank), gram, 0.0)
        packed = gram[:rank]
        for i in range(rank, LANES, rank):
            packed = packed + gram[i:i + rank]
        gram_ref[:, k:k + LANES] = packed


def first_update_kernel(w_ref, factor_ref, part_ref):
    part_ref[...] = mm(w_ref[...], factor_ref[...], 0, 0)


def update_kernel(gram_ref, p_ref, w_ref, part_ref, f_ref):
    rank = gram_ref.shape[0]
    for k in range(0, f_ref.shape[0], LANES):
        gram = jnp.concatenate([gram_ref[:, k:k + LANES]] * (LANES // rank), 0)
        gram = jnp.where(same_block(gram.shape, rank, rank), gram, 0.0)
        f_ref[k:k + LANES, :] = mm(gram, p_ref[k:k + LANES, :], 1, 0)
    part_ref[...] = mm(w_ref[...], f_ref[...], 0, 0)


def cores_kernel(rank, n_rows, at_ref, sent_ref, got_ref, here_ref, cores_ref, out_ref, in_ref):
    n = sent_ref.shape[0] - here_ref.shape[0]
    r = here_ref.shape[1]
    at = at_ref[0]

    def place(mine, p_ref, q_ref):
        one_hot = lax.broadcasted_iota(jnp.int32, (n_rows, r), 1) == (
            at * n_rows + lax.broadcasted_iota(jnp.int32, (n_rows, r), 0)
        )
        cols = mm(one_hot.astype(F32), p_ref[:n, :], 1, 1)
        group = LANES // rank
        size = group * n_rows
        for i, k in enumerate(range(0, n, LANES)):
            block = jnp.concatenate([cols[:, k:k + LANES]] * group, 0)
            block = jnp.where(same_block(block.shape, n_rows, rank), block, 0.0)
            cores_ref[i * size:(i + 1) * size, :] = mm(block, q_ref[k:k + LANES, :], 1, 0)
        here, away = (out_ref, in_ref) if mine else (in_ref, out_ref)
        here[...] = here_ref[...]
        away[...] = got_ref[n:, :]

    @pl.when(at % 2 == 0)
    def _():
        place(True, sent_ref, got_ref)

    @pl.when(at % 2 == 1)
    def _():
        place(False, got_ref, sent_ref)


def last_kernel(whole_ref, raw_ref, sent_ref, here_ref, x_ref, y_ref):
    n = y_ref.shape[0]
    half = here_ref.shape[0]
    sent_ref[:n, :] = factor_and_project(whole_ref, x_ref, y_ref)
    basis = mm(raw_ref[...], x_ref[...], 1, 1)
    here_ref[...] = basis[:half, :]
    sent_ref[n:, :] = basis[half:, :]


def call(kernel, shapes, args, scratch=(), scalars=0, out=jax.ShapeDtypeStruct):
    return pl.pallas_call(
        kernel,
        out_shape=[out(shape, F32) for shape in shapes],
        in_specs=[pl.BlockSpec(memory_space=pltpu.SMEM)] * scalars
        + [pl.BlockSpec(memory_space=pltpu.VMEM)] * (len(args) - scalars),
        out_specs=[pl.BlockSpec(memory_space=pltpu.VMEM)] * len(shapes),
        scratch_shapes=[pltpu.VMEM(shape, F32) for shape in scratch],
        compiler_params=pltpu.CompilerParams(vmem_limit_bytes=VMEM_BYTES),
    )(*args)


def exchange(chunks, axis, groups):
    return lax.all_to_all(chunks, axis, 0, 0, tiled=True, axis_index_groups=groups)


def scatter_sum(chunks, axis, groups):
    return jnp.sum(exchange(chunks, axis, groups), axis=0)


def gather(own, axis, groups):
    return exchange(jnp.broadcast_to(own[None], (len(groups[0]),) + own.shape), axis, groups)


def body(adapter_input_weight, adapter_output_weight, initial_output_basis, initial_input_basis):
    tenants, rank, feats = adapter_output_weight.shape
    r = initial_output_basis.shape[1]
    n_feat, n_tenant = lax.axis_size("feat"), lax.axis_size("tenant")
    chips = n_feat // 2
    core = lax.axis_index("feat") % 2
    same_core = [[2 * i + c for i in range(chips)] for c in range(2)]
    side = math.isqrt(chips)
    along_x = [[(y * side + x) * 2 + c for x in range(side)] for y in range(side) for c in range(2)]
    along_y = [[(y * side + x) * 2 + c for y in range(side)] for x in range(side) for c in range(2)]
    n_z = n_tenant // 2
    along_z = [[h * n_z + z for z in range(n_z)] for h in range(2)]
    swap_cores = [(i, i ^ 1) for i in range(n_feat)]
    swap_halves = [(i, (i + n_z) % n_tenant) for i in range(n_tenant)]
    mine = tenants // chips

    def pick(for_out, for_in):
        return jnp.where(core == 0, for_out, for_in)

    def to_partner(x):
        return lax.ppermute(x, "feat", swap_cores)

    w_out = adapter_output_weight.reshape(tenants * rank, feats)
    w_in = adapter_input_weight.reshape(tenants * rank, feats)
    sent = pick(
        jnp.concatenate([w_in, initial_input_basis], 0),
        jnp.concatenate([w_out, initial_output_basis], 0),
    )
    got = to_partner(sent)
    w = jnp.concatenate([pick(w_out, w_in), got[:tenants * rank]], 1)
    basis = jnp.concatenate([pick(initial_output_basis, initial_input_basis), got[tenants * rank:]], 0)

    n = tenants * rank
    own_rows = mine * rank

    partial = mm(w, basis, 1, 0).reshape(chips, own_rows, r)
    p, gram = call(
        functools.partial(first_gram_kernel, rank),
        [(own_rows, r), (own_rows, own_rows)],
        [exchange(partial, "feat", same_core)],
    )
    copies = call(
        first_factor_kernel, [(chips, own_rows, r)], [p, to_partner(gram)], out=pltpu.VMEM
    )[0]
    factor = exchange(copies, "feat", same_core).reshape(n, r)
    part = call(first_update_kernel, [(2 * feats, r)], [w, factor])[0]

    for step in range(ITERS):
        own = scatter_sum(part.reshape(n_z, 2 * feats // n_z, r), "tenant", along_z)
        own = own + lax.ppermute(own, "tenant", swap_halves)
        raw = gather(own, "tenant", along_z).reshape(2 * feats, r)
        chunk = (chips, 2 * own_rows + 3 * LANES // chips, LANES)
        own = scatter_sum(call(project_kernel, [chunk], [w, raw])[0], "feat", same_core)
        whole = gather(gather(own, "feat", along_y), "feat", along_x).reshape(chunk)
        scratch = [(r, r), (n, r)]
        if step < ITERS - 1:
            p, gram = call(
                functools.partial(middle_kernel, rank), [(n, r), (rank, n)], [whole], scratch
            )
            part = call(update_kernel, [(2 * feats, r)], [to_partner(gram), p, w], [(n, r)])[0]
    sent, here = call(last_kernel, [(n + feats, r), (feats, r)], [whole, raw], scratch)
    n_rows = r // n_feat
    cores, out_basis, in_basis = call(
        functools.partial(cores_kernel, rank, n_rows),
        [(tenants * n_rows, r), (feats, r), (feats, r)],
        [lax.axis_index("feat").reshape(1), sent, to_partner(sent), here],
        scalars=1,
    )
    return cores.reshape(tenants, n_rows, r), out_basis, in_basis


def solution(mesh):
    placed = (
        P("tenant", None, "feat"),
        P("tenant", None, "feat"),
        P("feat", None),
        P("feat", None),
    )
    return jax.shard_map(
        body,
        mesh=mesh,
        in_specs=placed,
        out_specs=(P("tenant", "feat", None), P("feat", None), P("feat", None)),
        check_vma=False,
    )
```
